32 devices in a mesh: px: 8 (over y, x, core), py: 4 (over z).
Axes of the slice: x: 2, y: 2, z: 4, core: 2. Of those that a mesh axis runs over, the one named last changes fastest.
Arguments:
- start_vecs: float32 [512, 64, 128], P(('px', 'py')), may hold values from -6 to 6
- local_tiles: bfloat16 [512, 4, 128, 128], P(('px', 'py')), may hold values from -0.078125 to 0.078125
- local_cols: int32 [512, 4], P(('px', 'py')), may hold values from 0 to 15
- halo_tiles: bfloat16 [512, 128, 128], P(('px', 'py')), may hold values from -0.078125 to 0.078125
- halo_slot: int32 [512], P(('px', 'py')), may hold values from 0 to 7
- boundary: int32 [128, 2], P(('px', 'py')), may hold values from 0 to 15
Outputs:
- filtered: float32 [512, 64, 128], P(('px', 'py'))
- gram_matrix: float32 [64, 64], replicated
The draws below stay inside these ranges and needn't reach their ends.
Inputs may be any that keep to these rules, and one draw needn't show every extreme that they name: `local_cols`: local block indices within the partition. `boundary`: local block indices within the partition.
All inputs are finite; a program needn't handle non-finite values.
Results may differ from the reference program's by a relative error of at most 0.0055.
Values may be sent and summed in bfloat16 or wider, within the bound.
A program may use at most 64 MiB of HBM per device.

```python
import math
import jax
import jax.numpy as jnp
from jax import lax

K = 64
BS = 128
RB = 16
TPR = 4
NB = 2
DEG = 9
NBLK = 512
ROWS = 65536
N_PX = 8
N_PY = 4
DEVICES = 32


def draw_start_vecs(key, part):
    key_own = jax.random.fold_in(key, 11)
    key_shared = jax.random.fold_in(key, 23)
    key_weight = jax.random.fold_in(key, 37)
    key_sign = jax.random.fold_in(key, 41)
    own_part = jax.random.normal(key_own, (NBLK, K, BS), jnp.float32)
    shared_field = jax.random.normal(key_shared, (NBLK, 1, BS), jnp.float32)
    magnitude = jnp.exp(jax.random.uniform(key_weight, (K,), jnp.float32, math.log(0.5), math.log(1.5)))
    sign_flip = (2 * jax.random.randint(key_sign, (K,), 0, 2) - 1).astype(jnp.float32)
    mixed = own_part + (sign_flip * magnitude)[None, :, None] * shared_field
    return jnp.clip(mixed, -6.0, 6.0)


def set_ends(values, rng, least, high):
    shape = values.shape
    spot = [jax.random.randint(jax.random.fold_in(rng, axis), (), 0, shape[axis]) for axis in range(len(shape))]
    values = values.at[tuple(spot)].set(least)
    longest = shape.index(max(shape))
    spot[longest] = (spot[longest] + 1) % shape[longest]
    return values.at[tuple(spot)].set(high)


def block_scale(key, dims, shards, low, top_value):
    level, own = 1.0, jax.random.fold_in(key, 6)
    for axis_at, parts in shards:
        heights = jnp.exp(jax.random.uniform(jax.random.fold_in(own, axis_at), (parts,), jnp.float32, low / len(shards), top_value / len(shards)))
        level = level * jnp.repeat(heights, dims[axis_at] // parts).reshape([-1 if axis == axis_at else 1 for axis in range(len(dims))])
    return level


def bell_draw(key, shape, scale, limit, split=(), held_as=jnp.bfloat16):
    factor_of = block_scale(key, shape, split, -0.22, 0.18) if split else 1.0
    entries = jax.random.normal(key, shape, jnp.float32) * scale * factor_of
    return jnp.minimum(jnp.maximum(entries, -limit), limit).astype(held_as)


def setup_inputs(seed: int = 0) -> dict:
    key_list = jax.random.split(jax.random.key(seed), 7)
    start_vecs = draw_start_vecs(jax.random.fold_in(key_list[6], 71), 0)
    local_tiles = bell_draw(key_list[1], (NBLK, TPR, BS, BS), (8 * BS * (TPR + 1)) ** -0.5, 0.078125, ((0, 32),))
    local_cols = set_ends(jax.random.randint(key_list[2], (NBLK, TPR), 0, RB), jax.random.fold_in(key_list[2], 1), 0, RB - 1).astype(jnp.int32)
    halo_tiles = bell_draw(key_list[3], (NBLK, BS, BS), (8 * BS * (TPR + 1)) ** -0.5, 0.078125, ((0, 32),))
    halo_slot = set_ends(jax.random.randint(key_list[4], (NBLK,), 0, 4 * NB), jax.random.fold_in(key_list[4], 1), 0, (4 * NB) - 1).astype(jnp.int32)
    boundary = set_ends(jax.random.randint(key_list[5], (4 * DEVICES, NB), 0, RB), jax.random.fold_in(key_list[5], 1), 0, RB - 1).astype(jnp.int32)
    return {"start_vecs": start_vecs, "local_tiles": local_tiles, "local_cols": local_cols, "halo_tiles": halo_tiles, "halo_slot": halo_slot, "boundary": boundary}


def reference(start_vecs, local_tiles, local_cols, halo_tiles, halo_slot, boundary):
    tiles_dev = local_tiles.reshape(DEVICES, RB, TPR, BS, BS)
    cols_dev = local_cols.reshape(DEVICES, RB, TPR)
    halo_dev = halo_tiles.reshape(DEVICES, RB, BS, BS)
    slots_dev = halo_slot.reshape(DEVICES, RB)
    bound_dev = boundary.reshape(DEVICES, 4, NB)

    def per_device(pieces):
        blocks_one, recv_one, tile_set, col_set, halo_set, slot_set = pieces
        gathered = blocks_one[col_set].astype(jnp.float32)
        product = jnp.einsum('rtkj,rtij->rki', gathered, tile_set.astype(jnp.float32))
        coupled = jnp.einsum('rkj,rij->rki', recv_one[slot_set].astype(jnp.float32), halo_set.astype(jnp.float32))
        return product + coupled

    def operator_apply(current):
        rounded = current.astype(jnp.bfloat16)
        outgoing = jax.vmap(lambda blocks_one, picks: blocks_one[picks])(rounded, bound_dev)
        grid_view = outgoing.reshape(N_PX, N_PY, 4, NB, K, BS)
        received = jnp.concatenate([jnp.roll(grid_view[:, :, 0], 1, 0), jnp.roll(grid_view[:, :, 1], -1, 0), jnp.roll(grid_view[:, :, 2], 1, 1), jnp.roll(grid_view[:, :, 3], -1, 1)], axis=2)
        received = received.reshape(DEVICES, 4 * NB, K, BS)
        return lax.map(per_device, (rounded, received, tiles_dev, cols_dev, halo_dev, slots_dev))
    previous = start_vecs.reshape(DEVICES, RB, K, BS)
    current = operator_apply(previous)
    for degree_step in range(DEG - 1):
        previous, current = (current, 2.0 * operator_apply(current) - previous)
    squares = lax.optimization_barrier(jnp.sum(current * current, axis=(0, 1, 3)))
    scales = lax.rsqrt(squares / ROWS + 1e-06)
    filtered = current * scales[None, None, :, None]
    gram_matrix = jnp.einsum('drkj,drlj->kl', filtered, filtered, precision=lax.Precision.HIGHEST) / ROWS
    return (filtered.reshape(NBLK, K, BS), gram_matrix)
```

```python
import functools

import jax
import jax.numpy as jnp
from jax import lax
from jax.experimental import pallas as pl
from jax.experimental.pallas import tpu as pltpu
from jax.sharding import PartitionSpec as P

DEG = 9
MESH = pl.DeviceIdType.MESH
NT = (((1,), (1,)), ((), ()))


def dot_nt(a, b):
    return lax.dot_general(a, b, NT, preferred_element_type=jnp.float32)


def filter_kernel(
    n_px, n_py, cols, slots, bnd, start_hbm, tiles_hbm, halo_hbm, y_hbm, g_out,
    y, vb, acc, tiles, halo, snd, rcv, cur, stk, gx, gy,
    in_sem, out_sem, snd_sem, rcv_sem, gx_snd, gx_rcv, gy_snd, gy_rcv,
):
    rb, tpr = tiles.shape[0], tiles.shape[1]
    nb = bnd.shape[1]
    i, j = lax.axis_index("px"), lax.axis_index("py")
    targets = (
        {"px": lax.rem(i + 1, n_px)},
        {"px": lax.rem(i + n_px - 1, n_px)},
        {"py": lax.rem(j + 1, n_py)},
        {"py": lax.rem(j + n_py - 1, n_py)},
    )

    load_start = pltpu.make_async_copy(start_hbm, y.at[0], in_sem.at[0])
    load_tiles = pltpu.make_async_copy(tiles_hbm, tiles, in_sem.at[1])
    load_halo = pltpu.make_async_copy(halo_hbm, halo, in_sem.at[2])
    load_start.start()
    load_tiles.start()
    load_halo.start()

    barrier = pltpu.get_barrier_semaphore()
    for off in range(1, n_px):
        pl.semaphore_signal(
            barrier, inc=1, device_id={"px": lax.rem(i + off, n_px)}, device_id_type=MESH
        )
    for off in range(1, n_py):
        pl.semaphore_signal(
            barrier, inc=1, device_id={"py": lax.rem(j + off, n_py)}, device_id_type=MESH
        )

    def exchange(step, d):
        rows = pl.ds(d * nb, nb)
        return pltpu.make_async_remote_copy(
            src_ref=snd.at[step, rows],
            dst_ref=rcv.at[step, rows],
            send_sem=snd_sem.at[step, d],
            recv_sem=rcv_sem.at[step, d],
            device_id=targets[d],
            device_id_type=MESH,
        )

    def local_product():
        for r in range(rb):
            gathered = jnp.concatenate([vb[cols[r, t]] for t in range(tpr)], axis=1)
            weights = jnp.concatenate([tiles[r, t] for t in range(tpr)], axis=1)
            acc[r] = dot_nt(gathered, weights)

    load_start.wait()
    vb[...] = y[0].astype(jnp.bfloat16)
    y[1] = jnp.zeros_like(y[1])
    for d in (3, 2, 1, 0):
        for b in range(nb):
            snd[0, d * nb + b] = vb[bnd[d, b]]
    pl.semaphore_wait(barrier, n_px + n_py - 2)
    for d in (3, 2, 1, 0):
        exchange(0, d).start()
    load_tiles.wait()
    load_halo.wait()
    local_product()

    def receive(step):
        for d in range(4):
            exchange(step, d).wait_recv()
        cur[...] = rcv[step]

    def next_rows(row, factor, older):
        coupled = dot_nt(cur[slots[row]], halo[row])
        return factor * (acc[row] + coupled) - y[older, row]

    def advance(step, carry):
        older = lax.rem(step + 1, 2)
        factor = jnp.where(step == 0, 1.0, 2.0).astype(jnp.float32)
        receive(step)
        for d in (3, 2, 1, 0):
            for b in range(nb):
                snd[step + 1, d * nb + b] = next_rows(bnd[d, b], factor, older).astype(jnp.bfloat16)
            exchange(step + 1, d).start()
        for r in range(rb):
            value = next_rows(r, factor, older)
            y[older, r] = value
            vb[r] = value.astype(jnp.bfloat16)
        local_product()
        return carry

    lax.fori_loop(0, DEG - 1, advance, 0)

    last, older = DEG - 1, DEG % 2
    receive(last)
    k, bs = y.shape[2], y.shape[3]
    for r in range(rb):
        value = next_rows(r, 2.0, older)
        y[older, r] = value
        high = value.astype(jnp.bfloat16)
        stk[0:k, r * bs:(r + 1) * bs] = high
        stk[k:2 * k, r * bs:(r + 1) * bs] = (value - high.astype(jnp.float32)).astype(jnp.bfloat16)
    store_y = pltpu.make_async_copy(y.at[older], y_hbm, out_sem)
    store_y.start()
    both = dot_nt(stk[...], stk[...])
    both = both[0:k] + both[k:2 * k]
    raw = both[:, 0:k] + both[:, k:2 * k]
    half = k // 2

    def all_sum(part, buf, axis, here, count, send_sems, recv_sems):
        buf[here] = part
        copies = []
        for off in range(1, count):
            copy = pltpu.make_async_remote_copy(
                src_ref=buf.at[here],
                dst_ref=buf.at[here],
                send_sem=send_sems.at[off],
                recv_sem=recv_sems.at[here],
                device_id={axis: lax.rem(here + off, count)},
                device_id_type=MESH,
            )
            copy.start()
            copies.append(copy)
        for off in range(1, count):
            other = lax.rem(here + off, count)
            pltpu.make_async_remote_copy(
                src_ref=buf.at[other],
                dst_ref=buf.at[other],
                send_sem=send_sems.at[off],
                recv_sem=recv_sems.at[other],
                device_id={axis: other},
                device_id_type=MESH,
            ).wait_recv()
        total = buf[0]
        for other in range(1, count):
            total = total + buf[other]
        return total, copies

    packed = jnp.concatenate([raw[0:half], raw[half:k]], axis=1)
    row_sum, copies_x = all_sum(packed, gx, "px", i, n_px, gx_snd, gx_rcv)
    total, copies_y = all_sum(row_sum, gy, "py", j, n_py, gy_snd, gy_rcv)
    g_out[...] = total

    for copy in copies_x + copies_y:
        copy.wait_send()

    def drain(step, carry):
        for d in range(4):
            exchange(step, d).wait_send()
        return carry

    lax.fori_loop(0, DEG, drain, 0)
    store_y.wait()


def scale_kernel(total_rows, y_ref, g_ref, f_ref, gram_ref):
    half = g_ref.shape[0]
    k = 2 * half
    g = g_ref[...]
    raw = jnp.concatenate([g[:, 0:k], g[:, k:2 * k]], axis=0)
    on_diag = lax.broadcasted_iota(jnp.int32, (k, k), 0) == lax.broadcasted_iota(
        jnp.int32, (k, k), 1
    )
    diag = jnp.where(on_diag, raw, 0.0)
    scale_col = lax.rsqrt(jnp.sum(diag, axis=1, keepdims=True) / total_rows + 1e-06)
    scale_row = lax.rsqrt(jnp.sum(diag, axis=0, keepdims=True) / total_rows + 1e-06)
    gram = raw * scale_col * scale_row / total_rows
    gram_ref[...] = jnp.where((scale_col == 0.0) | (scale_row == 0.0), 0.0, gram)
    f_ref[...] = y_ref[...] * scale_col[None]


def shards(n_px, n_py, start_vecs, local_tiles, local_cols, halo_tiles, halo_slot, boundary):
    rb, k, bs = start_vecs.shape
    nb = boundary.shape[1]
    total_rows = rb * bs * n_px * n_py
    f32, bf16 = jnp.float32, jnp.bfloat16
    smem = pl.BlockSpec(memory_space=pltpu.SMEM)
    vmem = pl.BlockSpec(memory_space=pltpu.VMEM)
    anywhere = pl.BlockSpec(memory_space=pl.ANY)
    dma = pltpu.SemaphoreType.DMA
    flops = 2 * DEG * rb * (local_cols.shape[1] + 1) * k * bs * bs
    vecs, gram_sum = pl.pallas_call(
        functools.partial(filter_kernel, n_px, n_py),
        out_shape=(
            jax.ShapeDtypeStruct((rb, k, bs), f32),
            jax.ShapeDtypeStruct((k // 2, 2 * k), f32),
        ),
        in_specs=[smem, smem, smem, anywhere, anywhere, anywhere],
        out_specs=(anywhere, vmem),
        scratch_shapes=[
            pltpu.VMEM((2, rb, k, bs), f32),
            pltpu.VMEM((rb, k, bs), bf16),
            pltpu.VMEM((rb, k, bs), f32),
            pltpu.VMEM(local_tiles.shape, bf16),
            pltpu.VMEM(halo_tiles.shape, bf16),
            pltpu.VMEM((DEG, 4 * nb, k, bs), bf16),
            pltpu.VMEM((DEG, 4 * nb, k, bs), bf16),
            pltpu.VMEM((4 * nb, k, bs), bf16),
            pltpu.VMEM((2 * k, rb * bs), bf16),
            pltpu.VMEM((n_px, k // 2, 2 * k), f32),
            pltpu.VMEM((n_py, k // 2, 2 * k), f32),
            dma((3,)),
            dma,
            dma((DEG, 4)),
            dma((DEG, 4)),
            dma((n_px,)),
            dma((n_px,)),
            dma((n_py,)),
            dma((n_py,)),
        ],
        compiler_params=pltpu.CompilerParams(
            collective_id=0, has_side_effects=True, vmem_limit_bytes=48 * 1024 * 1024
        ),
        cost_estimate=pl.CostEstimate(
            flops=flops, bytes_accessed=4 * 1024 * 1024, transcendentals=0
        ),
    )(local_cols, halo_slot, boundary, start_vecs, local_tiles, halo_tiles)
    return pl.pallas_call(
        functools.partial(scale_kernel, total_rows),
        out_shape=(
            jax.ShapeDtypeStruct((rb, k, bs), f32),
            jax.ShapeDtypeStruct((k, k), f32),
        ),
        in_specs=[vmem, vmem],
        out_specs=(vmem, vmem),
        cost_estimate=pl.CostEstimate(
            flops=rb * k * bs, bytes_accessed=2 * 4 * rb * k * bs, transcendentals=k
        ),
    )(vecs, gram_sum)


def solution(mesh):
    return jax.shard_map(
        functools.partial(shards, mesh.shape["px"], mesh.shape["py"]),
        mesh=mesh,
        in_specs=(
            P(("px", "py"), None, None),
            P(("px", "py"), None, None, None),
            P(("px", "py"), None),
            P(("px", "py"), None, None),
            P(("px", "py")),
            P(("px", "py"), None),
        ),
        out_specs=(P(("px", "py"), None, None), P()),
        check_vma=False,
    )
```

```python
import functools

import jax
import jax.numpy as jnp
from jax import lax
from jax.experimental import pallas as pl
from jax.experimental.pallas import tpu as pltpu
from jax.sharding import PartitionSpec as P

DEG = 9
VMEM_BYTES = 64 * 1024 * 1024
CHUNKS = 4
MESH = pl.DeviceIdType.MESH
NT = (((1,), (1,)), ((), ()))


def dot_nt(a, b):
    return lax.dot_general(a, b, NT, preferred_element_type=jnp.float32)


def dot(a, b):
    return jnp.dot(a, b, preferred_element_type=jnp.float32)


def filter_kernel(
    n_px, n_py, cols, slots, bnd, start_hbm, tiles_hbm, halo_hbm, y_hbm, g_out,
    y, vb, acc, tiles, halo, tiles_t, halo_t, snd, rcv, cur, stk, gx, gy,
    in_sem, out_sem, snd_sem, rcv_sem, gx_snd, gx_rcv, gy_snd, gy_rcv,
):
    rb, tpr = tiles.shape[0], tiles.shape[1]
    nb, bs = bnd.shape[0], tiles.shape[3]
    i, j = lax.axis_index("px"), lax.axis_index("py")
    targets = (
        {"px": lax.rem(i + 1, n_px)},
        {"px": lax.rem(i + n_px - 1, n_px)},
        {"py": lax.rem(j + 1, n_py)},
        {"py": lax.rem(j + n_py - 1, n_py)},
    )

    load_start = pltpu.make_async_copy(start_hbm, y.at[0], in_sem.at[0])
    load_tiles = pltpu.make_async_copy(tiles_hbm, tiles, in_sem.at[1])
    load_halo = pltpu.make_async_copy(halo_hbm, halo, in_sem.at[2])
    load_start.start()
    load_tiles.start()
    load_halo.start()

    barrier = pltpu.get_barrier_semaphore()
    for off in range(1, n_px):
        pl.semaphore_signal(
            barrier, inc=1, device_id={"px": lax.rem(i + off, n_px)}, device_id_type=MESH
        )
    for off in range(1, n_py):
        pl.semaphore_signal(
            barrier, inc=1, device_id={"py": lax.rem(j + off, n_py)}, device_id_type=MESH
        )

    def exchange(step, d):
        rows = pl.ds(d * nb, nb)
        return pltpu.make_async_remote_copy(
            src_ref=snd.at[step, rows],
            dst_ref=rcv.at[step, rows],
            send_sem=snd_sem.at[step, d],
            recv_sem=rcv_sem.at[step, d],
            device_id=targets[d],
            device_id_type=MESH,
        )

    def local_product():
        for r in range(rb):
            gathered = jnp.concatenate([vb[cols[t, r]] for t in range(tpr)], axis=1)
            acc[r] = dot(gathered, tiles_t[r])

    load_start.wait()
    vb[...] = y[0].astype(jnp.bfloat16)
    y[1] = jnp.zeros_like(y[1])
    for d in (3, 2, 1, 0):
        for b in range(nb):
            snd[0, d * nb + b] = vb[bnd[b, d]]
    pl.semaphore_wait(barrier, n_px + n_py - 2)
    for d in (3, 2, 1, 0):
        exchange(0, d).start()
    load_tiles.wait()
    for r in range(rb):
        for t in range(tpr):
            tiles_t[r, t * bs:(t + 1) * bs] = tiles[r, t].T
    local_product()
    load_halo.wait()
    for r in range(rb):
        halo_t[r] = halo[r].T

    def receive(step):
        for d in range(4):
            exchange(step, d).wait_recv()
        cur[...] = rcv[step]

    def next_rows(row, factor, older):
        coupled = dot(cur[slots[row]], halo_t[row])
        return factor * (acc[row] + coupled) - y[older, row]

    def advance(step, carry):
        older = lax.rem(step + 1, 2)
        factor = jnp.where(step == 0, 1.0, 2.0).astype(jnp.float32)
        receive(step)
        for d in (3, 2, 1, 0):
            for b in range(nb):
                snd[step + 1, d * nb + b] = next_rows(bnd[b, d], factor, older).astype(jnp.bfloat16)
            exchange(step + 1, d).start()
        for r in range(rb):
            value = next_rows(r, factor, older)
            y[older, r] = value
            vb[r] = value.astype(jnp.bfloat16)
        local_product()
        return carry

    lax.fori_loop(0, DEG - 1, advance, 0)

    last, older = DEG - 1, DEG % 2
    receive(last)
    k = y.shape[2]
    for r in range(rb):
        value = next_rows(r, 2.0, older)
        y[older, r] = value
        high = value.astype(jnp.bfloat16)
        stk[0:k, r * bs:(r + 1) * bs] = high
        stk[k:2 * k, r * bs:(r + 1) * bs] = (value - high.astype(jnp.float32)).astype(jnp.bfloat16)
    store_y = pltpu.make_async_copy(y.at[older], y_hbm, out_sem)
    store_y.start()
    both = dot_nt(stk[...], stk[...])
    both = both[0:k] + both[k:2 * k]
    raw = both[:, 0:k] + both[:, k:2 * k]
    half = k // 2

    def all_sum(part, buf, axis, here, count, send_sems, recv_sems):
        buf[here] = part
        copies = []
        for off in range(1, count):
            copy = pltpu.make_async_remote_copy(
                src_ref=buf.at[here],
                dst_ref=buf.at[here],
                send_sem=send_sems.at[off],
                recv_sem=recv_sems.at[here],
                device_id={axis: lax.rem(here + off, count)},
                device_id_type=MESH,
            )
            copy.start()
            copies.append(copy)
        for off in range(1, count):
            other = lax.rem(here + off, count)
            pltpu.make_async_remote_copy(
                src_ref=buf.at[other],
                dst_ref=buf.at[other],
                send_sem=send_sems.at[off],
                recv_sem=recv_sems.at[other],
                device_id={axis: other},
                device_id_type=MESH,
            ).wait_recv()
        total = buf[0]
        for other in range(1, count):
            total = total + buf[other]
        return total, copies

    packed = jnp.concatenate([raw[0:half], raw[half:k]], axis=1)
    row_sum, copies_x = all_sum(packed, gx, "px", i, n_px, gx_snd, gx_rcv)
    total, copies_y = all_sum(row_sum, gy, "py", j, n_py, gy_snd, gy_rcv)
    g_out[...] = total

    for copy in copies_x + copies_y:
        copy.wait_send()

    def drain(step, carry):
        for d in range(4):
            exchange(step, d).wait_send()
        return carry

    lax.fori_loop(0, DEG, drain, 0)
    store_y.wait()


def scale_kernel(total_rows, y_hbm, g_ref, f_hbm, gram_ref, y, f, in_sem, out_sem):
    rows = y.shape[0] // CHUNKS
    parts = [pl.ds(c * rows, rows) for c in range(CHUNKS)]
    loads = [pltpu.make_async_copy(y_hbm.at[p], y.at[p], in_sem.at[c]) for c, p in enumerate(parts)]
    stores = [pltpu.make_async_copy(f.at[p], f_hbm.at[p], out_sem.at[c]) for c, p in enumerate(parts)]
    for load in loads:
        load.start()
    half = g_ref.shape[0]
    k = 2 * half
    g = g_ref[...]
    raw = jnp.concatenate([g[:, 0:k], g[:, k:2 * k]], axis=0)
    on_diag = lax.broadcasted_iota(jnp.int32, (k, k), 0) == lax.broadcasted_iota(
        jnp.int32, (k, k), 1
    )
    diag = jnp.where(on_diag, raw, 0.0)
    scale_col = lax.rsqrt(jnp.sum(diag, axis=1, keepdims=True) / total_rows + 1e-06)
    for c, p in enumerate(parts):
        loads[c].wait()
        f[p] = y[p] * scale_col[None]
        stores[c].start()
    scale_row = lax.rsqrt(jnp.sum(diag, axis=0, keepdims=True) / total_rows + 1e-06)
    gram = raw * scale_col * scale_row / total_rows
    gram_ref[...] = jnp.where((scale_col == 0.0) | (scale_row == 0.0), 0.0, gram)
    for store in stores:
        store.wait()


def shards(n_px, n_py, start_vecs, local_tiles, local_cols, halo_tiles, halo_slot, boundary):
    rb, k, bs = start_vecs.shape
    nb = boundary.shape[1]
    total_rows = rb * bs * n_px * n_py
    f32, bf16 = jnp.float32, jnp.bfloat16
    smem = pl.BlockSpec(memory_space=pltpu.SMEM)
    vmem = pl.BlockSpec(memory_space=pltpu.VMEM)
    anywhere = pl.BlockSpec(memory_space=pl.ANY)
    dma = pltpu.SemaphoreType.DMA
    flops = 2 * DEG * rb * (local_cols.shape[1] + 1) * k * bs * bs
    vecs, gram_sum = pl.pallas_call(
        functools.partial(filter_kernel, n_px, n_py),
        out_shape=(
            jax.ShapeDtypeStruct((rb, k, bs), f32),
            jax.ShapeDtypeStruct((k // 2, 2 * k), f32),
        ),
        in_specs=[smem, smem, smem, anywhere, anywhere, anywhere],
        out_specs=(anywhere, vmem),
        scratch_shapes=[
            pltpu.VMEM((2, rb, k, bs), f32),
            pltpu.VMEM((rb, k, bs), bf16),
            pltpu.VMEM((rb, k, bs), f32),
            pltpu.VMEM(local_tiles.shape, bf16),
            pltpu.VMEM(halo_tiles.shape, bf16),
            pltpu.VMEM((rb, local_cols.shape[1] * bs, bs), bf16),
            pltpu.VMEM(halo_tiles.shape, bf16),
            pltpu.VMEM((DEG, 4 * nb, k, bs), bf16),
            pltpu.VMEM((DEG, 4 * nb, k, bs), bf16),
            pltpu.VMEM((4 * nb, k, bs), bf16),
            pltpu.VMEM((2 * k, rb * bs), bf16),
            pltpu.VMEM((n_px, k // 2, 2 * k), f32),
            pltpu.VMEM((n_py, k // 2, 2 * k), f32),
            dma((3,)),
            dma,
            dma((DEG, 4)),
            dma((DEG, 4)),
            dma((n_px,)),
            dma((n_px,)),
            dma((n_py,)),
            dma((n_py,)),
        ],
        compiler_params=pltpu.CompilerParams(
            collective_id=0, has_side_effects=True, vmem_limit_bytes=VMEM_BYTES
        ),
        cost_estimate=pl.CostEstimate(
            flops=flops, bytes_accessed=4 * 1024 * 1024, transcendentals=0
        ),
    )(local_cols.T, halo_slot, boundary.T, start_vecs, local_tiles, halo_tiles)
    return pl.pallas_call(
        functools.partial(scale_kernel, total_rows),
        out_shape=(
            jax.ShapeDtypeStruct((rb, k, bs), f32),
            jax.ShapeDtypeStruct((k, k), f32),
        ),
        in_specs=[anywhere, vmem],
        out_specs=(anywhere, vmem),
        scratch_shapes=[
            pltpu.VMEM((rb, k, bs), f32),
            pltpu.VMEM((rb, k, bs), f32),
            dma((CHUNKS,)),
            dma((CHUNKS,)),
        ],
        compiler_params=pltpu.CompilerParams(vmem_limit_bytes=VMEM_BYTES),
        cost_estimate=pl.CostEstimate(
            flops=rb * k * bs, bytes_accessed=2 * 4 * rb * k * bs, transcendentals=k
        ),
    )(vecs, gram_sum)


def solution(mesh):
    return jax.shard_map(
        functools.partial(shards, mesh.shape["px"], mesh.shape["py"]),
        mesh=mesh,
        in_specs=(
            P(("px", "py"), None, None),
            P(("px", "py"), None, None, None),
            P(("px", "py"), None),
            P(("px", "py"), None, None),
            P(("px", "py")),
            P(("px", "py"), None),
        ),
        out_specs=(P(("px", "py"), None, None), P()),
        check_vma=False,
    )
```

```python
import functools

import jax
import jax.numpy as jnp
from jax import lax
from jax.experimental import pallas as pl
from jax.experimental.pallas import tpu as pltpu
from jax.sharding import PartitionSpec as P

DEG = 9
VMEM_BYTES = 64 * 1024 * 1024
LAG = 4
MESH = pl.DeviceIdType.MESH
NT = (((1,), (1,)), ((), ()))


def dot_nt(a, b):
    return lax.dot_general(a, b, NT, preferred_element_type=jnp.float32)


def dot(a, b):
    return jnp.dot(a, b, preferred_element_type=jnp.float32)


def filter_kernel(
    n_px, n_py, cols, slots, bnd, start_hbm, tiles_hbm, halo_hbm, y_hbm, scale_out, gram_out,
    y, vb, acc, tiles, halo, tiles_t, halo_t, snd, rcv, cur, stk, gx, gy,
    in_sem, out_sem, snd_sem, rcv_sem, gx_snd, gx_rcv, gy_snd, gy_rcv,
):
    rb, tpr = tiles.shape[0], tiles.shape[1]
    nb, bs = bnd.shape[0], tiles.shape[3]
    i, j = lax.axis_index("px"), lax.axis_index("py")
    targets = (
        {"px": lax.rem(i + 1, n_px)},
        {"px": lax.rem(i + n_px - 1, n_px)},
        {"py": lax.rem(j + 1, n_py)},
        {"py": lax.rem(j + n_py - 1, n_py)},
    )

    load_start = pltpu.make_async_copy(start_hbm, y.at[0], in_sem.at[0])
    load_tiles = pltpu.make_async_copy(tiles_hbm, tiles, in_sem.at[1])
    load_halo = pltpu.make_async_copy(halo_hbm, halo, in_sem.at[2])
    load_start.start()
    load_tiles.start()
    load_halo.start()

    barrier = pltpu.get_barrier_semaphore()
    for off in range(1, n_px):
        pl.semaphore_signal(
            barrier, inc=1, device_id={"px": lax.rem(i + off, n_px)}, device_id_type=MESH
        )
    for off in range(1, n_py):
        pl.semaphore_signal(
            barrier, inc=1, device_id={"py": lax.rem(j + off, n_py)}, device_id_type=MESH
        )

    def exchange(step, d):
        rows = pl.ds(d * nb, nb)
        return pltpu.make_async_remote_copy(
            src_ref=snd.at[step, rows],
            dst_ref=rcv.at[step, rows],
            send_sem=snd_sem.at[step, d],
            recv_sem=rcv_sem.at[step, d],
            device_id=targets[d],
            device_id_type=MESH,
        )

    def lagged(make, keep):
        pending = []
        for r in range(rb):
            pending.append((r, make(r)))
            if len(pending) > LAG:
                keep(*pending.pop(0))
        for row, value in pending:
            keep(row, value)

    def local_product():
        def make(r):
            gathered = jnp.concatenate([vb[cols[t, r]] for t in range(tpr)], axis=1)
            return dot(gathered, tiles_t[r])

        def keep(r, value):
            acc[r] = value

        lagged(make, keep)

    load_start.wait()
    vb[...] = y[0].astype(jnp.bfloat16)
    y[1] = jnp.zeros_like(y[1])
    for d in (3, 2, 1, 0):
        for b in range(nb):
            snd[0, d * nb + b] = vb[bnd[b, d]]
    pl.semaphore_wait(barrier, n_px + n_py - 2)
    for d in (3, 2, 1, 0):
        exchange(0, d).start()
    load_tiles.wait()
    for r in range(rb):
        for t in range(tpr):
            tiles_t[r, t * bs:(t + 1) * bs] = tiles[r, t].T
    local_product()
    load_halo.wait()
    for r in range(rb):
        halo_t[r] = halo[r].T

    def receive(step):
        for d in range(4):
            exchange(step, d).wait_recv()
        cur[...] = rcv[step]

    def next_rows(row, factor, older):
        coupled = dot(cur[slots[row]], halo_t[row])
        return factor * (acc[row] + coupled) - y[older, row]

    def advance(step, carry):
        older = lax.rem(step + 1, 2)
        factor = jnp.where(step == 0, 1.0, 2.0).astype(jnp.float32)
        receive(step)
        for pair in ((3, 2), (1, 0)):
            blocks = [
                next_rows(bnd[b, d], factor, older).astype(jnp.bfloat16)
                for d in pair for b in range(nb)
            ]
            for at, d in enumerate(pair):
                for b in range(nb):
                    snd[step + 1, d * nb + b] = blocks[at * nb + b]
            for d in pair:
                exchange(step + 1, d).start()

        def keep(r, value):
            y[older, r] = value
            vb[r] = value.astype(jnp.bfloat16)

        lagged(lambda r: next_rows(r, factor, older), keep)
        local_product()
        return carry

    lax.fori_loop(0, DEG - 1, advance, 0)

    last, older = DEG - 1, DEG % 2
    receive(last)
    k = y.shape[2]

    def keep_last(r, value):
        y[older, r] = value
        high = value.astype(jnp.bfloat16)
        stk[0:k, r * bs:(r + 1) * bs] = high
        stk[k:2 * k, r * bs:(r + 1) * bs] = (value - high.astype(jnp.float32)).astype(jnp.bfloat16)

    lagged(lambda r: next_rows(r, 2.0, older), keep_last)
    store_y = pltpu.make_async_copy(y.at[older], y_hbm, out_sem)
    store_y.start()
    both = dot_nt(stk[...], stk[...])
    both = both[0:k] + both[k:2 * k]
    raw = both[:, 0:k] + both[:, k:2 * k]
    half = k // 2

    def all_sum(part, buf, axis, here, count, send_sems, recv_sems):
        buf[here] = part
        copies = []
        for off in range(1, count):
            copy = pltpu.make_async_remote_copy(
                src_ref=buf.at[here],
                dst_ref=buf.at[here],
                send_sem=send_sems.at[off],
                recv_sem=recv_sems.at[here],
                device_id={axis: lax.rem(here + off, count)},
                device_id_type=MESH,
            )
            copy.start()
            copies.append(copy)
        for off in range(1, count):
            other = lax.rem(here + off, count)
            pltpu.make_async_remote_copy(
                src_ref=buf.at[other],
                dst_ref=buf.at[other],
                send_sem=send_sems.at[off],
                recv_sem=recv_sems.at[other],
                device_id={axis: other},
                device_id_type=MESH,
            ).wait_recv()
        total = buf[0]
        for other in range(1, count):
            total = total + buf[other]
        return total, copies

    packed = jnp.concatenate([raw[0:half], raw[half:k]], axis=1)
    row_sum, copies_x = all_sum(packed, gx, "px", i, n_px, gx_snd, gx_rcv)
    total, copies_y = all_sum(row_sum, gy, "py", j, n_py, gy_snd, gy_rcv)
    raw = jnp.concatenate([total[:, 0:k], total[:, k:2 * k]], axis=0)
    on_diag = lax.broadcasted_iota(jnp.int32, (k, k), 0) == lax.broadcasted_iota(
        jnp.int32, (k, k), 1
    )
    diag = jnp.where(on_diag, raw, 0.0)
    total_rows = rb * bs * n_px * n_py
    scale_col = lax.rsqrt(jnp.sum(diag, axis=1, keepdims=True) / total_rows + 1e-06)
    scale_row = lax.rsqrt(jnp.sum(diag, axis=0, keepdims=True) / total_rows + 1e-06)
    scale_out[...] = jnp.broadcast_to(scale_col, scale_out.shape)
    gram = raw * scale_col * scale_row / total_rows
    gram_out[...] = jnp.where((scale_col == 0.0) | (scale_row == 0.0), 0.0, gram)

    for copy in copies_x + copies_y:
        copy.wait_send()

    def drain(step, carry):
        for d in range(4):
            exchange(step, d).wait_send()
        return carry

    lax.fori_loop(0, DEG, drain, 0)
    store_y.wait()


def shards(n_px, n_py, start_vecs, local_tiles, local_cols, halo_tiles, halo_slot, boundary):
    rb, k, bs = start_vecs.shape
    nb = boundary.shape[1]
    f32, bf16 = jnp.float32, jnp.bfloat16
    smem = pl.BlockSpec(memory_space=pltpu.SMEM)
    vmem = pl.BlockSpec(memory_space=pltpu.VMEM)
    anywhere = pl.BlockSpec(memory_space=pl.ANY)
    dma = pltpu.SemaphoreType.DMA
    flops = 2 * DEG * rb * (local_cols.shape[1] + 1) * k * bs * bs
    vecs, scale, gram = pl.pallas_call(
        functools.partial(filter_kernel, n_px, n_py),
        out_shape=(
            jax.ShapeDtypeStruct((rb, k, bs), f32),
            jax.ShapeDtypeStruct((k, bs), f32),
            jax.ShapeDtypeStruct((k, k), f32),
        ),
        in_specs=[smem, smem, smem, anywhere, anywhere, anywhere],
        out_specs=(anywhere, vmem, vmem),
        scratch_shapes=[
            pltpu.VMEM((2, rb, k, bs), f32),
            pltpu.VMEM((rb, k, bs), bf16),
            pltpu.VMEM((rb, k, bs), f32),
            pltpu.VMEM(local_tiles.shape, bf16),
            pltpu.VMEM(halo_tiles.shape, bf16),
            pltpu.VMEM((rb, local_cols.shape[1] * bs, bs), bf16),
            pltpu.VMEM(halo_tiles.shape, bf16),
            pltpu.VMEM((DEG, 4 * nb, k, bs), bf16),
            pltpu.VMEM((DEG, 4 * nb, k, bs), bf16),
            pltpu.VMEM((4 * nb, k, bs), bf16),
            pltpu.VMEM((2 * k, rb * bs), bf16),
            pltpu.VMEM((n_px, k // 2, 2 * k), f32),
            pltpu.VMEM((n_py, k // 2, 2 * k), f32),
            dma((3,)),
            dma,
            dma((DEG, 4)),
            dma((DEG, 4)),
            dma((n_px,)),
            dma((n_px,)),
            dma((n_py,)),
            dma((n_py,)),
        ],
        compiler_params=pltpu.CompilerParams(
            collective_id=0, has_side_effects=True, vmem_limit_bytes=VMEM_BYTES
        ),
        cost_estimate=pl.CostEstimate(
            flops=flops, bytes_accessed=4 * 1024 * 1024, transcendentals=0
        ),
    )(local_cols.T, halo_slot, boundary.T, start_vecs, local_tiles, halo_tiles)
    return vecs * scale[None], gram


def solution(mesh):
    return jax.shard_map(
        functools.partial(shards, mesh.shape["px"], mesh.shape["py"]),
        mesh=mesh,
        in_specs=(
            P(("px", "py"), None, None),
            P(("px", "py"), None, None, None),
            P(("px", "py"), None),
            P(("px", "py"), None, None),
            P(("px", "py")),
            P(("px", "py"), None),
        ),
        out_specs=(P(("px", "py"), None, None), P()),
        check_vma=False,
    )
```

```python
import functools

import jax
import jax.numpy as jnp
from jax import lax
from jax.experimental import pallas as pl
from jax.experimental.pallas import tpu as pltpu
from jax.sharding import PartitionSpec as P

DEG = 9
VMEM_BYTES = 64 * 1024 * 1024
LAG = 4
CHUNKS = 4
MESH = pl.DeviceIdType.MESH
NT = (((1,), (1,)), ((), ()))


def dot_nt(a, b):
    return lax.dot_general(a, b, NT, preferred_element_type=jnp.float32)


def dot(a, b):
    return jnp.dot(a, b, preferred_element_type=jnp.float32)


def filter_kernel(
    n_px, n_py, cols, slots, bnd, start_hbm, tiles_hbm, halo_hbm, y_hbm, g_out,
    y, vb, acc, tiles, halo, tiles_t, halo_t, snd, rcv, cur, stk, gx, gy,
    in_sem, out_sem, snd_sem, rcv_sem, gx_snd, gx_rcv, gy_snd, gy_rcv,
):
    rb, tpr = tiles.shape[0], tiles.shape[1]
    nb, bs = bnd.shape[0], tiles.shape[3]
    i, j = lax.axis_index("px"), lax.axis_index("py")
    targets = (
        {"px": lax.rem(i + 1, n_px)},
        {"px": lax.rem(i + n_px - 1, n_px)},
        {"py": lax.rem(j + 1, n_py)},
        {"py": lax.rem(j + n_py - 1, n_py)},
    )

    load_start = pltpu.make_async_copy(start_hbm, y.at[0], in_sem.at[0])
    load_tiles = pltpu.make_async_copy(tiles_hbm, tiles, in_sem.at[1])
    load_halo = pltpu.make_async_copy(halo_hbm, halo, in_sem.at[2])
    load_start.start()
    load_tiles.start()
    load_halo.start()

    barrier = pltpu.get_barrier_semaphore()
    for off in range(1, n_px):
        pl.semaphore_signal(
            barrier, inc=1, device_id={"px": lax.rem(i + off, n_px)}, device_id_type=MESH
        )
    for off in range(1, n_py):
        pl.semaphore_signal(
            barrier, inc=1, device_id={"py": lax.rem(j + off, n_py)}, device_id_type=MESH
        )

    long_way = jnp.where(j == n_py - 1, 2, 3)
    short_way = 5 - long_way
    step_py = jnp.where(j == n_py - 1, 1, n_py - 1)
    py_targets = ({"py": lax.rem(j + step_py, n_py)}, {"py": lax.rem(j + n_py - step_py, n_py)})
    order = (
        ((long_way, py_targets[0]),),
        ((1, targets[1]), (0, targets[0])),
        ((short_way, py_targets[1]),),
    )

    def exchange(step, d, target=None):
        rows = pl.ds(d * nb, nb)
        return pltpu.make_async_remote_copy(
            src_ref=snd.at[step, rows],
            dst_ref=rcv.at[step, rows],
            send_sem=snd_sem.at[step, d],
            recv_sem=rcv_sem.at[step, d],
            device_id=targets[d] if target is None else target,
            device_id_type=MESH,
        )

    def lagged(make, keep):
        pending = []
        for r in range(rb):
            pending.append((r, make(r)))
            if len(pending) > LAG:
                keep(*pending.pop(0))
        for row, value in pending:
            keep(row, value)

    def local_product():
        def make(r):
            gathered = jnp.concatenate([vb[cols[t, r]] for t in range(tpr)], axis=1)
            return dot(gathered, tiles_t[r])

        def keep(r, value):
            acc[r] = value

        lagged(make, keep)

    load_start.wait()
    vb[...] = y[0].astype(jnp.bfloat16)
    y[1] = jnp.zeros_like(y[1])
    for d in range(4):
        for b in range(nb):
            snd[0, d * nb + b] = vb[bnd[b, d]]
    pl.semaphore_wait(barrier, n_px + n_py - 2)
    for group in order:
        for d, target in group:
            exchange(0, d, target).start()
    load_tiles.wait()
    for r in range(rb):
        for t in range(tpr):
            tiles_t[r, t * bs:(t + 1) * bs] = tiles[r, t].T
    local_product()
    load_halo.wait()
    for r in range(rb):
        halo_t[r] = halo[r].T

    def receive(step):
        for d in range(4):
            exchange(step, d).wait_recv()
        cur[...] = rcv[step]

    def next_rows(row, factor, older):
        coupled = dot(cur[slots[row]], halo_t[row])
        return factor * (acc[row] + coupled) - y[older, row]

    def advance(step, carry):
        older = lax.rem(step + 1, 2)
        factor = jnp.where(step == 0, 1.0, 2.0).astype(jnp.float32)
        receive(step)
        for group in order:
            blocks = [
                next_rows(bnd[b, d], factor, older).astype(jnp.bfloat16)
                for d, _ in group for b in range(nb)
            ]
            for at, (d, _) in enumerate(group):
                for b in range(nb):
                    snd[step + 1, d * nb + b] = blocks[at * nb + b]
            for d, target in group:
                exchange(step + 1, d, target).start()

        def keep(r, value):
            y[older, r] = value
            vb[r] = value.astype(jnp.bfloat16)

        lagged(lambda r: next_rows(r, factor, older), keep)
        local_product()
        return carry

    lax.fori_loop(0, DEG - 1, advance, 0)

    last, older = DEG - 1, DEG % 2
    receive(last)
    k = y.shape[2]

    def keep_last(r, value):
        y[older, r] = value
        high = value.astype(jnp.bfloat16)
        stk[0:k, r * bs:(r + 1) * bs] = high
        stk[k:2 * k, r * bs:(r + 1) * bs] = (value - high.astype(jnp.float32)).astype(jnp.bfloat16)

    lagged(lambda r: next_rows(r, 2.0, older), keep_last)
    store_y = pltpu.make_async_copy(y.at[older], y_hbm, out_sem)
    store_y.start()
    both = dot_nt(stk[...], stk[...])
    both = both[0:k] + both[k:2 * k]
    raw = both[:, 0:k] + both[:, k:2 * k]
    half = k // 2

    def all_sum(part, buf, axis, here, count, send_sems, recv_sems):
        buf[here] = part
        copies = []
        for off in range(1, count):
            copy = pltpu.make_async_remote_copy(
                src_ref=buf.at[here],
                dst_ref=buf.at[here],
                send_sem=send_sems.at[off],
                recv_sem=recv_sems.at[here],
                device_id={axis: lax.rem(here + off, count)},
                device_id_type=MESH,
            )
            copy.start()
            copies.append(copy)
        for off in range(1, count):
            other = lax.rem(here + off, count)
            pltpu.make_async_remote_copy(
                src_ref=buf.at[other],
                dst_ref=buf.at[other],
                send_sem=send_sems.at[off],
                recv_sem=recv_sems.at[other],
                device_id={axis: other},
                device_id_type=MESH,
            ).wait_recv()
        total = buf[0]
        for other in range(1, count):
            total = total + buf[other]
        return total, copies

    packed = jnp.concatenate([raw[0:half], raw[half:k]], axis=1)
    row_sum, copies_x = all_sum(packed, gx, "px", i, n_px, gx_snd, gx_rcv)
    total, copies_y = all_sum(row_sum, gy, "py", j, n_py, gy_snd, gy_rcv)
    g_out[...] = total

    for copy in copies_x + copies_y:
        copy.wait_send()

    def drain(step, carry):
        for d in range(4):
            exchange(step, d).wait_send()
        return carry

    lax.fori_loop(0, DEG, drain, 0)
    store_y.wait()


def scale_kernel(total_rows, y_hbm, g_hbm, f_hbm, gram_hbm, y, f, g_ref, gram_ref, in_sem, out_sem):
    rows = y.shape[0] // CHUNKS
    parts = [pl.ds(c * rows, rows) for c in range(CHUNKS)]
    loads = [pltpu.make_async_copy(y_hbm.at[p], y.at[p], in_sem.at[c]) for c, p in enumerate(parts)]
    stores = [pltpu.make_async_copy(f.at[p], f_hbm.at[p], out_sem.at[c]) for c, p in enumerate(parts)]
    load_g = pltpu.make_async_copy(g_hbm, g_ref, in_sem.at[CHUNKS])
    store_g = pltpu.make_async_copy(gram_ref, gram_hbm, out_sem.at[CHUNKS])
    load_g.start()
    for load in loads:
        load.start()
    load_g.wait()
    half = g_ref.shape[0]
    k = 2 * half
    g = g_ref[...]
    raw = jnp.concatenate([g[:, 0:k], g[:, k:2 * k]], axis=0)
    on_diag = lax.broadcasted_iota(jnp.int32, (k, k), 0) == lax.broadcasted_iota(
        jnp.int32, (k, k), 1
    )
    diag = jnp.where(on_diag, raw, 0.0)
    scale_col = lax.rsqrt(jnp.sum(diag, axis=1, keepdims=True) / total_rows + 1e-06)
    scale_row = lax.rsqrt(jnp.sum(diag, axis=0, keepdims=True) / total_rows + 1e-06)
    gram = raw * scale_col * scale_row / total_rows
    gram_ref[...] = jnp.where((scale_col == 0.0) | (scale_row == 0.0), 0.0, gram)
    store_g.start()
    for c, p in enumerate(parts):
        loads[c].wait()
        f[p] = y[p] * scale_col[None]
        stores[c].start()
    for store in stores:
        store.wait()
    store_g.wait()


def shards(n_px, n_py, start_vecs, local_tiles, local_cols, halo_tiles, halo_slot, boundary):
    rb, k, bs = start_vecs.shape
    nb = boundary.shape[1]
    total_rows = rb * bs * n_px * n_py
    f32, bf16 = jnp.float32, jnp.bfloat16
    smem = pl.BlockSpec(memory_space=pltpu.SMEM)
    vmem = pl.BlockSpec(memory_space=pltpu.VMEM)
    anywhere = pl.BlockSpec(memory_space=pl.ANY)
    dma = pltpu.SemaphoreType.DMA
    flops = 2 * DEG * rb * (local_cols.shape[1] + 1) * k * bs * bs
    vecs, gram_sum = pl.pallas_call(
        functools.partial(filter_kernel, n_px, n_py),
        out_shape=(
            jax.ShapeDtypeStruct((rb, k, bs), f32),
            jax.ShapeDtypeStruct((k // 2, 2 * k), f32),
        ),
        in_specs=[smem, smem, smem, anywhere, anywhere, anywhere],
        out_specs=(anywhere, vmem),
        scratch_shapes=[
            pltpu.VMEM((2, rb, k, bs), f32),
            pltpu.VMEM((rb, k, bs), bf16),
            pltpu.VMEM((rb, k, bs), f32),
            pltpu.VMEM(local_tiles.shape, bf16),
            pltpu.VMEM(halo_tiles.shape, bf16),
            pltpu.VMEM((rb, local_cols.shape[1] * bs, bs), bf16),
            pltpu.VMEM(halo_tiles.shape, bf16),
            pltpu.VMEM((DEG, 4 * nb, k, bs), bf16),
            pltpu.VMEM((DEG, 4 * nb, k, bs), bf16),
            pltpu.VMEM((4 * nb, k, bs), bf16),
            pltpu.VMEM((2 * k, rb * bs), bf16),
            pltpu.VMEM((n_px, k // 2, 2 * k), f32),
            pltpu.VMEM((n_py, k // 2, 2 * k), f32),
            dma((3,)),
            dma,
            dma((DEG, 4)),
            dma((DEG, 4)),
            dma((n_px,)),
            dma((n_px,)),
            dma((n_py,)),
            dma((n_py,)),
        ],
        compiler_params=pltpu.CompilerParams(
            collective_id=0, has_side_effects=True, vmem_limit_bytes=VMEM_BYTES
        ),
        cost_estimate=pl.CostEstimate(
            flops=flops, bytes_accessed=4 * 1024 * 1024, transcendentals=0
        ),
    )(local_cols.T, halo_slot, boundary.T, start_vecs, local_tiles, halo_tiles)
    return pl.pallas_call(
        functools.partial(scale_kernel, total_rows),
        out_shape=(
            jax.ShapeDtypeStruct((rb, k, bs), f32),
            jax.ShapeDtypeStruct((k, k), f32),
        ),
        in_specs=[anywhere, anywhere],
        out_specs=(anywhere, anywhere),
        scratch_shapes=[
            pltpu.VMEM((rb, k, bs), f32),
            pltpu.VMEM((rb, k, bs), f32),
            pltpu.VMEM((k // 2, 2 * k), f32),
            pltpu.VMEM((k, k), f32),
            dma((CHUNKS + 1,)),
            dma((CHUNKS + 1,)),
        ],
        compiler_params=pltpu.CompilerParams(vmem_limit_bytes=VMEM_BYTES),
        cost_estimate=pl.CostEstimate(
            flops=rb * k * bs, bytes_accessed=2 * 4 * rb * k * bs, transcendentals=k
        ),
    )(vecs, gram_sum)


def solution(mesh):
    return jax.shard_map(
        functools.partial(shards, mesh.shape["px"], mesh.shape["py"]),
        mesh=mesh,
        in_specs=(
            P(("px", "py"), None, None),
            P(("px", "py"), None, None, None),
            P(("px", "py"), None),
            P(("px", "py"), None, None),
            P(("px", "py")),
            P(("px", "py"), None),
        ),
        out_specs=(P(("px", "py"), None, None), P()),
        check_vma=False,
    )
```

```python
import functools

import jax
import jax.numpy as jnp
from jax import lax
from jax.experimental import pallas as pl
from jax.experimental.pallas import tpu as pltpu
from jax.sharding import PartitionSpec as P

DEG = 9
VMEM_BYTES = 64 * 1024 * 1024
LAG = 4
CHUNKS = 4
MESH = pl.DeviceIdType.MESH
NT = (((1,), (1,)), ((), ()))


def dot_nt(a, b):
    return lax.dot_general(a, b, NT, preferred_element_type=jnp.float32)


def dot(a, b):
    return jnp.dot(a, b, preferred_element_type=jnp.float32)


def filter_kernel(
    n_px, n_py, cols, slots, bnd, start_hbm, tiles_hbm, halo_hbm, y_hbm, g_out,
    y, vb, acc, tiles, halo, tiles_t, halo_t, snd, rcv, cur, stk, gx, gy,
    in_sem, out_sem, snd_sem, rcv_sem, gx_snd, gx_rcv, gy_snd, gy_rcv,
):
    rb, tpr = tiles.shape[0], tiles.shape[1]
    nb, bs = bnd.shape[0], tiles.shape[3]
    i, j = lax.axis_index("px"), lax.axis_index("py")
    targets = (
        {"px": lax.rem(i + 1, n_px)},
        {"px": lax.rem(i + n_px - 1, n_px)},
        {"py": lax.rem(j + 1, n_py)},
        {"py": lax.rem(j + n_py - 1, n_py)},
    )

    load_start = pltpu.make_async_copy(start_hbm, y.at[0], in_sem.at[0])
    load_tiles = pltpu.make_async_copy(tiles_hbm, tiles, in_sem.at[1])
    load_halo = pltpu.make_async_copy(halo_hbm, halo, in_sem.at[2])
    load_start.start()
    load_tiles.start()
    load_halo.start()

    barrier = pltpu.get_barrier_semaphore()
    for off in range(1, n_px):
        pl.semaphore_signal(
            barrier, inc=1, device_id={"px": lax.rem(i + off, n_px)}, device_id_type=MESH
        )
    for off in range(1, n_py):
        pl.semaphore_signal(
            barrier, inc=1, device_id={"py": lax.rem(j + off, n_py)}, device_id_type=MESH
        )

    forward_first = (j == n_py - 1) | ((j > 0) & (2 * j < n_py))
    long_way = jnp.where(forward_first, 2, 3)
    short_way = 5 - long_way
    step_py = jnp.where(forward_first, 1, n_py - 1)
    py_targets = ({"py": lax.rem(j + step_py, n_py)}, {"py": lax.rem(j + n_py - step_py, n_py)})
    order = (
        ((long_way, py_targets[0]),),
        ((1, targets[1]), (0, targets[0])),
        ((short_way, py_targets[1]),),
    )

    def exchange(step, d, target=None):
        rows = pl.ds(d * nb, nb)
        return pltpu.make_async_remote_copy(
            src_ref=snd.at[step, rows],
            dst_ref=rcv.at[step, rows],
            send_sem=snd_sem.at[step, d],
            recv_sem=rcv_sem.at[step, d],
            device_id=targets[d] if target is None else target,
            device_id_type=MESH,
        )

    def lagged(make, keep):
        pending = []
        for r in range(rb):
            pending.append((r, make(r)))
            if len(pending) > LAG:
                keep(*pending.pop(0))
        for row, value in pending:
            keep(row, value)

    def local_product():
        def make(r):
            gathered = jnp.concatenate([vb[cols[t, r]] for t in range(tpr)], axis=1)
            return dot(gathered, tiles_t[r])

        def keep(r, value):
            acc[r] = value

        lagged(make, keep)

    load_start.wait()
    vb[...] = y[0].astype(jnp.bfloat16)
    y[1] = jnp.zeros_like(y[1])
    for d in range(4):
        for b in range(nb):
            snd[0, d * nb + b] = vb[bnd[b, d]]
    pl.semaphore_wait(barrier, n_px + n_py - 2)
    for group in order:
        for d, target in group:
            exchange(0, d, target).start()
    load_tiles.wait()
    for r in range(rb):
        for t in range(tpr):
            tiles_t[r, t * bs:(t + 1) * bs] = tiles[r, t].T
    local_product()
    load_halo.wait()
    for r in range(rb):
        halo_t[r] = halo[r].T

    def receive(step):
        for d in range(4):
            exchange(step, d).wait_recv()
        cur[...] = rcv[step]

    def next_rows(row, factor, older):
        coupled = dot(cur[slots[row]], halo_t[row])
        return factor * (acc[row] + coupled) - y[older, row]

    def advance(step, carry):
        older = lax.rem(step + 1, 2)
        factor = jnp.where(step == 0, 1.0, 2.0).astype(jnp.float32)
        receive(step)
        for group in order:
            blocks = [
                next_rows(bnd[b, d], factor, older).astype(jnp.bfloat16)
                for d, _ in group for b in range(nb)
            ]
            for at, (d, _) in enumerate(group):
                for b in range(nb):
                    snd[step + 1, d * nb + b] = blocks[at * nb + b]
            for d, target in group:
                exchange(step + 1, d, target).start()

        def keep(r, value):
            y[older, r] = value
            vb[r] = value.astype(jnp.bfloat16)

        lagged(lambda r: next_rows(r, factor, older), keep)
        local_product()
        return carry

    lax.fori_loop(0, DEG - 1, advance, 0)

    last, older = DEG - 1, DEG % 2
    receive(last)
    k = y.shape[2]

    def keep_last(r, value):
        y[older, r] = value
        high = value.astype(jnp.bfloat16)
        stk[0:k, r * bs:(r + 1) * bs] = high
        stk[k:2 * k, r * bs:(r + 1) * bs] = (value - high.astype(jnp.float32)).astype(jnp.bfloat16)

    lagged(lambda r: next_rows(r, 2.0, older), keep_last)
    store_y = pltpu.make_async_copy(y.at[older], y_hbm, out_sem)
    store_y.start()
    both = dot_nt(stk[...], stk[...])
    both = both[0:k] + both[k:2 * k]
    raw = both[:, 0:k] + both[:, k:2 * k]
    half = k // 2

    def all_sum(part, buf, axis, here, count, send_sems, recv_sems):
        buf[here] = part
        copies = []
        for off in range(1, count):
            down, up = count - off, off - 1
            peer = jnp.where(
                2 * here < count,
                down - jnp.where(down <= here, 1, 0),
                up + jnp.where(up >= here, 1, 0),
            )
            copy = pltpu.make_async_remote_copy(
                src_ref=buf.at[here],
                dst_ref=buf.at[here],
                send_sem=send_sems.at[off],
                recv_sem=recv_sems.at[here],
                device_id={axis: peer},
                device_id_type=MESH,
            )
            copy.start()
            copies.append(copy)
        for off in range(1, count):
            other = lax.rem(here + off, count)
            pltpu.make_async_remote_copy(
                src_ref=buf.at[other],
                dst_ref=buf.at[other],
                send_sem=send_sems.at[off],
                recv_sem=recv_sems.at[other],
                device_id={axis: other},
                device_id_type=MESH,
            ).wait_recv()
        total = buf[0]
        for other in range(1, count):
            total = total + buf[other]
        return total, copies

    packed = jnp.concatenate([raw[0:half], raw[half:k]], axis=1)
    row_sum, copies_x = all_sum(packed, gx, "px", i, n_px, gx_snd, gx_rcv)
    total, copies_y = all_sum(row_sum, gy, "py", j, n_py, gy_snd, gy_rcv)
    g_out[...] = total

    for copy in copies_x + copies_y:
        copy.wait_send()

    def drain(step, carry):
        for d in range(4):
            exchange(step, d).wait_send()
        return carry

    lax.fori_loop(0, DEG, drain, 0)
    store_y.wait()


def scale_kernel(total_rows, y_hbm, g_hbm, f_hbm, gram_hbm, y, f, g_ref, gram_ref, in_sem, out_sem):
    rows = y.shape[0] // CHUNKS
    parts = [pl.ds(c * rows, rows) for c in range(CHUNKS)]
    loads = [pltpu.make_async_copy(y_hbm.at[p], y.at[p], in_sem.at[c]) for c, p in enumerate(parts)]
    stores = [pltpu.make_async_copy(f.at[p], f_hbm.at[p], out_sem.at[c]) for c, p in enumerate(parts)]
    load_g = pltpu.make_async_copy(g_hbm, g_ref, in_sem.at[CHUNKS])
    store_g = pltpu.make_async_copy(gram_ref, gram_hbm, out_sem.at[CHUNKS])
    load_g.start()
    for load in loads:
        load.start()
    load_g.wait()
    half = g_ref.shape[0]
    k = 2 * half
    g = g_ref[...]
    raw = jnp.concatenate([g[:, 0:k], g[:, k:2 * k]], axis=0)
    on_diag = lax.broadcasted_iota(jnp.int32, (k, k), 0) == lax.broadcasted_iota(
        jnp.int32, (k, k), 1
    )
    diag = jnp.where(on_diag, raw, 0.0)
    scale_col = lax.rsqrt(jnp.sum(diag, axis=1, keepdims=True) / total_rows + 1e-06)
    scale_row = lax.rsqrt(jnp.sum(diag, axis=0, keepdims=True) / total_rows + 1e-06)
    gram = raw * scale_col * scale_row / total_rows
    gram_ref[...] = jnp.where((scale_col == 0.0) | (scale_row == 0.0), 0.0, gram)
    store_g.start()
    for c, p in enumerate(parts):
        loads[c].wait()
        f[p] = y[p] * scale_col[None]
        stores[c].start()
    for store in stores:
        store.wait()
    store_g.wait()


def shards(n_px, n_py, start_vecs, local_tiles, local_cols, halo_tiles, halo_slot, boundary):
    rb, k, bs = start_vecs.shape
    nb = boundary.shape[1]
    total_rows = rb * bs * n_px * n_py
    f32, bf16 = jnp.float32, jnp.bfloat16
    smem = pl.BlockSpec(memory_space=pltpu.SMEM)
    vmem = pl.BlockSpec(memory_space=pltpu.VMEM)
    anywhere = pl.BlockSpec(memory_space=pl.ANY)
    dma = pltpu.SemaphoreType.DMA
    flops = 2 * DEG * rb * (local_cols.shape[1] + 1) * k * bs * bs
    vecs, gram_sum = pl.pallas_call(
        functools.partial(filter_kernel, n_px, n_py),
        out_shape=(
            jax.ShapeDtypeStruct((rb, k, bs), f32),
            jax.ShapeDtypeStruct((k // 2, 2 * k), f32),
        ),
        in_specs=[smem, smem, smem, anywhere, anywhere, anywhere],
        out_specs=(anywhere, vmem),
        scratch_shapes=[
            pltpu.VMEM((2, rb, k, bs), f32),
            pltpu.VMEM((rb, k, bs), bf16),
            pltpu.VMEM((rb, k, bs), f32),
            pltpu.VMEM(local_tiles.shape, bf16),
            pltpu.VMEM(halo_tiles.shape, bf16),
            pltpu.VMEM((rb, local_cols.shape[1] * bs, bs), bf16),
            pltpu.VMEM(halo_tiles.shape, bf16),
            pltpu.VMEM((DEG, 4 * nb, k, bs), bf16),
            pltpu.VMEM((DEG, 4 * nb, k, bs), bf16),
            pltpu.VMEM((4 * nb, k, bs), bf16),
            pltpu.VMEM((2 * k, rb * bs), bf16),
            pltpu.VMEM((n_px, k // 2, 2 * k), f32),
            pltpu.VMEM((n_py, k // 2, 2 * k), f32),
            dma((3,)),
            dma,
            dma((DEG, 4)),
            dma((DEG, 4)),
            dma((n_px,)),
            dma((n_px,)),
            dma((n_py,)),
            dma((n_py,)),
        ],
        compiler_params=pltpu.CompilerParams(
            collective_id=0, has_side_effects=True, vmem_limit_bytes=VMEM_BYTES
        ),
        cost_estimate=pl.CostEstimate(
            flops=flops, bytes_accessed=4 * 1024 * 1024, transcendentals=0
        ),
    )(local_cols.T, halo_slot, boundary.T, start_vecs, local_tiles, halo_tiles)
    return pl.pallas_call(
        functools.partial(scale_kernel, total_rows),
        out_shape=(
            jax.ShapeDtypeStruct((rb, k, bs), f32),
            jax.ShapeDtypeStruct((k, k), f32),
        ),
        in_specs=[anywhere, anywhere],
        out_specs=(anywhere, anywhere),
        scratch_shapes=[
            pltpu.VMEM((rb, k, bs), f32),
            pltpu.VMEM((rb, k, bs), f32),
            pltpu.VMEM((k // 2, 2 * k), f32),
            pltpu.VMEM((k, k), f32),
            dma((CHUNKS + 1,)),
            dma((CHUNKS + 1,)),
        ],
        compiler_params=pltpu.CompilerParams(vmem_limit_bytes=VMEM_BYTES),
        cost_estimate=pl.CostEstimate(
            flops=rb * k * bs, bytes_accessed=2 * 4 * rb * k * bs, transcendentals=k
        ),
    )(vecs, gram_sum)


def solution(mesh):
    return jax.shard_map(
        functools.partial(shards, mesh.shape["px"], mesh.shape["py"]),
        mesh=mesh,
        in_specs=(
            P(("px", "py"), None, None),
            P(("px", "py"), None, None, None),
            P(("px", "py"), None),
            P(("px", "py"), None, None),
            P(("px", "py")),
            P(("px", "py"), None),
        ),
        out_specs=(P(("px", "py"), None, None), P()),
        check_vma=False,
    )
```

```python
import functools

import jax
import jax.numpy as jnp
from jax import lax
from jax.experimental import pallas as pl
from jax.experimental.pallas import tpu as pltpu
from jax.sharding import PartitionSpec as P

DEG = 9
VMEM_BYTES = 64 * 1024 * 1024
LAG = 4
CHUNKS = 4
MESH = pl.DeviceIdType.MESH
NT = (((1,), (1,)), ((), ()))


def dot_nt(a, b):
    return lax.dot_general(a, b, NT, preferred_element_type=jnp.float32)


def filter_kernel(
    n_px, n_py, cols, slots, bnd, start_hbm, tiles_hbm, halo_hbm, y_hbm, g_out,
    y, vb, acc, tiles, halo, snd, rcv, cur, stk, gx, gy,
    in_sem, out_sem, snd_sem, rcv_sem, gx_snd, gx_rcv, gy_snd, gy_rcv,
):
    rb, tpr = tiles.shape[0], tiles.shape[1]
    nb, bs = bnd.shape[0], tiles.shape[3]
    i, j = lax.axis_index("px"), lax.axis_index("py")
    targets = (
        {"px": lax.rem(i + 1, n_px)},
        {"px": lax.rem(i + n_px - 1, n_px)},
        {"py": lax.rem(j + 1, n_py)},
        {"py": lax.rem(j + n_py - 1, n_py)},
    )

    load_start = pltpu.make_async_copy(start_hbm, y.at[0], in_sem.at[0])
    load_tiles = pltpu.make_async_copy(tiles_hbm, tiles, in_sem.at[1])
    load_halo = pltpu.make_async_copy(halo_hbm, halo, in_sem.at[2])
    load_start.start()
    load_tiles.start()
    load_halo.start()

    barrier = pltpu.get_barrier_semaphore()
    for off in range(1, n_px):
        pl.semaphore_signal(
            barrier, inc=1, device_id={"px": lax.rem(i + off, n_px)}, device_id_type=MESH
        )
    for off in range(1, n_py):
        pl.semaphore_signal(
            barrier, inc=1, device_id={"py": lax.rem(j + off, n_py)}, device_id_type=MESH
        )

    forward_first = (j == n_py - 1) | ((j > 0) & (2 * j < n_py))
    long_way = jnp.where(forward_first, 2, 3)
    short_way = 5 - long_way
    step_py = jnp.where(forward_first, 1, n_py - 1)
    py_targets = ({"py": lax.rem(j + step_py, n_py)}, {"py": lax.rem(j + n_py - step_py, n_py)})
    order = (
        ((long_way, py_targets[0]),),
        ((1, targets[1]), (0, targets[0])),
        ((short_way, py_targets[1]),),
    )

    def exchange(step, d, target=None):
        rows = pl.ds(d * nb, nb)
        return pltpu.make_async_remote_copy(
            src_ref=snd.at[step, rows],
            dst_ref=rcv.at[step, rows],
            send_sem=snd_sem.at[step, d],
            recv_sem=rcv_sem.at[step, d],
            device_id=targets[d] if target is None else target,
            device_id_type=MESH,
        )

    def lagged(make, keep):
        pending = []
        for r in range(rb):
            pending.append((r, make(r)))
            if len(pending) > LAG:
                keep(*pending.pop(0))
        for row, value in pending:
            keep(row, value)

    def local_product():
        def make(r):
            gathered = jnp.concatenate([vb[cols[t, r]] for t in range(tpr)], axis=1)
            weights = jnp.concatenate([tiles[r, t] for t in range(tpr)], axis=1)
            return dot_nt(gathered, weights)

        def keep(r, value):
            acc[r] = value

        lagged(make, keep)

    load_start.wait()
    for d in range(4):
        for b in range(nb):
            snd[0, d * nb + b] = y[0, bnd[b, d]].astype(jnp.bfloat16)
    pl.semaphore_wait(barrier, n_px + n_py - 2)
    for group in order:
        for d, target in group:
            exchange(0, d, target).start()
    vb[...] = y[0].astype(jnp.bfloat16)
    y[1] = jnp.zeros_like(y[1])
    load_tiles.wait()
    local_product()
    load_halo.wait()

    def receive(step):
        for d in range(4):
            exchange(step, d).wait_recv()
        cur[...] = rcv[step]

    def next_rows(row, factor, older):
        coupled = dot_nt(cur[slots[row]], halo[row])
        return factor * (acc[row] + coupled) - y[older, row]

    def advance(step, carry):
        older = lax.rem(step + 1, 2)
        factor = jnp.where(step == 0, 1.0, 2.0).astype(jnp.float32)
        receive(step)
        for group in order:
            blocks = [
                next_rows(bnd[b, d], factor, older).astype(jnp.bfloat16)
                for d, _ in group for b in range(nb)
            ]
            for at, (d, _) in enumerate(group):
                for b in range(nb):
                    snd[step + 1, d * nb + b] = blocks[at * nb + b]
            for d, target in group:
                exchange(step + 1, d, target).start()

        def keep(r, value):
            y[older, r] = value
            vb[r] = value.astype(jnp.bfloat16)

        lagged(lambda r: next_rows(r, factor, older), keep)
        local_product()
        return carry

    lax.fori_loop(0, DEG - 1, advance, 0)

    last, older = DEG - 1, DEG % 2
    receive(last)
    k = y.shape[2]

    def keep_last(r, value):
        y[older, r] = value
        high = value.astype(jnp.bfloat16)
        stk[0:k, r * bs:(r + 1) * bs] = high
        stk[k:2 * k, r * bs:(r + 1) * bs] = (value - high.astype(jnp.float32)).astype(jnp.bfloat16)

    lagged(lambda r: next_rows(r, 2.0, older), keep_last)
    store_y = pltpu.make_async_copy(y.at[older], y_hbm, out_sem)
    store_y.start()
    both = dot_nt(stk[...], stk[...])
    both = both[0:k] + both[k:2 * k]
    raw = both[:, 0:k] + both[:, k:2 * k]
    half = k // 2

    def all_sum(part, buf, axis, here, count, send_sems, recv_sems):
        buf[here] = part
        copies = []
        for off in range(1, count):
            down, up = count - off, off - 1
            peer = jnp.where(
                2 * here < count,
                down - jnp.where(down <= here, 1, 0),
                up + jnp.where(up >= here, 1, 0),
            )
            copy = pltpu.make_async_remote_copy(
                src_ref=buf.at[here],
                dst_ref=buf.at[here],
                send_sem=send_sems.at[off],
                recv_sem=recv_sems.at[here],
                device_id={axis: peer},
                device_id_type=MESH,
            )
            copy.start()
            copies.append(copy)
        for off in range(1, count):
            other = lax.rem(here + off, count)
            pltpu.make_async_remote_copy(
                src_ref=buf.at[other],
                dst_ref=buf.at[other],
                send_sem=send_sems.at[off],
                recv_sem=recv_sems.at[other],
                device_id={axis: other},
                device_id_type=MESH,
            ).wait_recv()
        total = buf[0]
        for other in range(1, count):
            total = total + buf[other]
        return total, copies

    packed = jnp.concatenate([raw[0:half], raw[half:k]], axis=1)
    row_sum, copies_x = all_sum(packed, gx, "px", i, n_px, gx_snd, gx_rcv)
    total, copies_y = all_sum(row_sum, gy, "py", j, n_py, gy_snd, gy_rcv)
    g_out[...] = total

    for copy in copies_x + copies_y:
        copy.wait_send()

    def drain(step, carry):
        for d in range(4):
            exchange(step, d).wait_send()
        return carry

    lax.fori_loop(0, DEG, drain, 0)
    store_y.wait()


def scale_kernel(total_rows, y_hbm, g_hbm, f_hbm, gram_hbm, y, f, g_ref, gram_ref, in_sem, out_sem):
    rows = y.shape[0] // CHUNKS
    parts = [pl.ds(c * rows, rows) for c in range(CHUNKS)]
    loads = [pltpu.make_async_copy(y_hbm.at[p], y.at[p], in_sem.at[c]) for c, p in enumerate(parts)]
    stores = [pltpu.make_async_copy(f.at[p], f_hbm.at[p], out_sem.at[c]) for c, p in enumerate(parts)]
    load_g = pltpu.make_async_copy(g_hbm, g_ref, in_sem.at[CHUNKS])
    store_g = pltpu.make_async_copy(gram_ref, gram_hbm, out_sem.at[CHUNKS])
    load_g.start()
    for load in loads:
        load.start()
    load_g.wait()
    half = g_ref.shape[0]
    k = 2 * half
    g = g_ref[...]
    raw = jnp.concatenate([g[:, 0:k], g[:, k:2 * k]], axis=0)
    on_diag = lax.broadcasted_iota(jnp.int32, (k, k), 0) == lax.broadcasted_iota(
        jnp.int32, (k, k), 1
    )
    diag = jnp.where(on_diag, raw, 0.0)
    scale_col = lax.rsqrt(jnp.sum(diag, axis=1, keepdims=True) / total_rows + 1e-06)
    scale_row = lax.rsqrt(jnp.sum(diag, axis=0, keepdims=True) / total_rows + 1e-06)
    gram = raw * scale_col * scale_row / total_rows
    gram_ref[...] = jnp.where((scale_col == 0.0) | (scale_row == 0.0), 0.0, gram)
    store_g.start()
    for c, p in enumerate(parts):
        loads[c].wait()
        f[p] = y[p] * scale_col[None]
        stores[c].start()
    for store in stores:
        store.wait()
    store_g.wait()


def shards(n_px, n_py, start_vecs, local_tiles, local_cols, halo_tiles, halo_slot, boundary):
    rb, k, bs = start_vecs.shape
    nb = boundary.shape[1]
    total_rows = rb * bs * n_px * n_py
    f32, bf16 = jnp.float32, jnp.bfloat16
    smem = pl.BlockSpec(memory_space=pltpu.SMEM)
    vmem = pl.BlockSpec(memory_space=pltpu.VMEM)
    anywhere = pl.BlockSpec(memory_space=pl.ANY)
    dma = pltpu.SemaphoreType.DMA
    flops = 2 * DEG * rb * (local_cols.shape[1] + 1) * k * bs * bs
    vecs, gram_sum = pl.pallas_call(
        functools.partial(filter_kernel, n_px, n_py),
        out_shape=(
            jax.ShapeDtypeStruct((rb, k, bs), f32),
            jax.ShapeDtypeStruct((k // 2, 2 * k), f32),
        ),
        in_specs=[smem, smem, smem, anywhere, anywhere, anywhere],
        out_specs=(anywhere, vmem),
        scratch_shapes=[
            pltpu.VMEM((2, rb, k, bs), f32),
            pltpu.VMEM((rb, k, bs), bf16),
            pltpu.VMEM((rb, k, bs), f32),
            pltpu.VMEM(local_tiles.shape, bf16),
            pltpu.VMEM(halo_tiles.shape, bf16),
            pltpu.VMEM((DEG, 4 * nb, k, bs), bf16),
            pltpu.VMEM((DEG, 4 * nb, k, bs), bf16),
            pltpu.VMEM((4 * nb, k, bs), bf16),
            pltpu.VMEM((2 * k, rb * bs), bf16),
            pltpu.VMEM((n_px, k // 2, 2 * k), f32),
            pltpu.VMEM((n_py, k // 2, 2 * k), f32),
            dma((3,)),
            dma,
            dma((DEG, 4)),
            dma((DEG, 4)),
            dma((n_px,)),
            dma((n_px,)),
            dma((n_py,)),
            dma((n_py,)),
        ],
        compiler_params=pltpu.CompilerParams(
            collective_id=0, has_side_effects=True, vmem_limit_bytes=VMEM_BYTES
        ),
        cost_estimate=pl.CostEstimate(
            flops=flops, bytes_accessed=4 * 1024 * 1024, transcendentals=0
        ),
    )(local_cols.T, halo_slot, boundary.T, start_vecs, local_tiles, halo_tiles)
    return pl.pallas_call(
        functools.partial(scale_kernel, total_rows),
        out_shape=(
            jax.ShapeDtypeStruct((rb, k, bs), f32),
            jax.ShapeDtypeStruct((k, k), f32),
        ),
        in_specs=[anywhere, anywhere],
        out_specs=(anywhere, anywhere),
        scratch_shapes=[
            pltpu.VMEM((rb, k, bs), f32),
            pltpu.VMEM((rb, k, bs), f32),
            pltpu.VMEM((k // 2, 2 * k), f32),
            pltpu.VMEM((k, k), f32),
            dma((CHUNKS + 1,)),
            dma((CHUNKS + 1,)),
        ],
        compiler_params=pltpu.CompilerParams(vmem_limit_bytes=VMEM_BYTES),
        cost_estimate=pl.CostEstimate(
            flops=rb * k * bs, bytes_accessed=2 * 4 * rb * k * bs, transcendentals=k
        ),
    )(vecs, gram_sum)


def solution(mesh):
    return jax.shard_map(
        functools.partial(shards, mesh.shape["px"], mesh.shape["py"]),
        mesh=mesh,
        in_specs=(
            P(("px", "py"), None, None),
            P(("px", "py"), None, None, None),
            P(("px", "py"), None),
            P(("px", "py"), None, None),
            P(("px", "py")),
            P(("px", "py"), None),
        ),
        out_specs=(P(("px", "py"), None, None), P()),
        check_vma=False,
    )
```

```python
import functools

import jax
import jax.numpy as jnp
from jax import lax
from jax.experimental import pallas as pl
from jax.experimental.pallas import tpu as pltpu
from jax.sharding import PartitionSpec as P

DEG = 9
VMEM_BYTES = 64 * 1024 * 1024
LAG = 4
CHUNKS = 4
MESH = pl.DeviceIdType.MESH
NT = (((1,), (1,)), ((), ()))


def dot_nt(a, b):
    return lax.dot_general(a, b, NT, preferred_element_type=jnp.float32)


def dot(a, b):
    return jnp.dot(a, b, preferred_element_type=jnp.float32)


def filter_kernel(
    n_px, n_py, cols, slots, bnd, start_hbm, tiles_hbm, halo_hbm, y_hbm, g_out,
    y, vb, acc, tiles, halo, tiles_t, halo_t, snd, rcv, cur, stk, gx, gy,
    in_sem, out_sem, snd_sem, rcv_sem, gx_snd, gx_rcv, gy_snd, gy_rcv,
):
    rb, tpr = tiles.shape[0], tiles.shape[1]
    nb, bs = bnd.shape[0], tiles.shape[3]
    i, j = lax.axis_index("px"), lax.axis_index("py")
    targets = (
        {"px": lax.rem(i + 1, n_px)},
        {"px": lax.rem(i + n_px - 1, n_px)},
        {"py": lax.rem(j + 1, n_py)},
        {"py": lax.rem(j + n_py - 1, n_py)},
    )

    load_start = pltpu.make_async_copy(start_hbm, y.at[0], in_sem.at[0])
    load_tiles = pltpu.make_async_copy(tiles_hbm, tiles, in_sem.at[1])
    load_halo = pltpu.make_async_copy(halo_hbm, halo, in_sem.at[2])
    load_start.start()
    load_tiles.start()
    load_halo.start()

    barrier = pltpu.get_barrier_semaphore()
    for off in range(1, n_px):
        pl.semaphore_signal(
            barrier, inc=1, device_id={"px": lax.rem(i + off, n_px)}, device_id_type=MESH
        )
    for off in range(1, n_py):
        pl.semaphore_signal(
            barrier, inc=1, device_id={"py": lax.rem(j + off, n_py)}, device_id_type=MESH
        )

    forward_first = (j == n_py - 1) | ((j > 0) & (2 * j < n_py))
    long_way = jnp.where(forward_first, 2, 3)
    short_way = 5 - long_way
    step_py = jnp.where(forward_first, 1, n_py - 1)
    py_targets = ({"py": lax.rem(j + step_py, n_py)}, {"py": lax.rem(j + n_py - step_py, n_py)})
    order = (
        ((long_way, py_targets[0]),),
        ((1, targets[1]), (0, targets[0])),
        ((short_way, py_targets[1]),),
    )

    def exchange(step, d, target=None):
        rows = pl.ds(d * nb, nb)
        return pltpu.make_async_remote_copy(
            src_ref=snd.at[step, rows],
            dst_ref=rcv.at[step, rows],
            send_sem=snd_sem.at[step, d],
            recv_sem=rcv_sem.at[step, d],
            device_id=targets[d] if target is None else target,
            device_id_type=MESH,
        )

    def lagged(make, keep):
        pending = []
        for r in range(rb):
            pending.append((r, make(r)))
            if len(pending) > LAG:
                keep(*pending.pop(0))
        for row, value in pending:
            keep(row, value)

    def local_product():
        def make(r):
            gathered = jnp.concatenate([vb[cols[t, r]] for t in range(tpr)], axis=1)
            return dot(gathered, tiles_t[r])

        def keep(r, value):
            acc[r] = value

        lagged(make, keep)

    load_start.wait()
    for d in range(4):
        for b in range(nb):
            snd[0, d * nb + b] = y[0, bnd[b, d]].astype(jnp.bfloat16)
    pl.semaphore_wait(barrier, n_px + n_py - 2)
    for group in order:
        for d, target in group:
            exchange(0, d, target).start()
    vb[...] = y[0].astype(jnp.bfloat16)
    y[1] = jnp.zeros_like(y[1])
    load_tiles.wait()
    for r in range(rb):
        for t in range(tpr):
            tiles_t[r, t * bs:(t + 1) * bs] = tiles[r, t].T
    local_product()
    load_halo.wait()
    for r in range(rb):
        halo_t[r] = halo[r].T

    def receive(step):
        for d in range(4):
            exchange(step, d).wait_recv()
        cur[...] = rcv[step]

    def next_rows(row, factor, older):
        coupled = dot(cur[slots[row]], halo_t[row])
        return factor * (acc[row] + coupled) - y[older, row]

    def advance(step, carry):
        older = lax.rem(step + 1, 2)
        factor = jnp.where(step == 0, 1.0, 2.0).astype(jnp.float32)
        receive(step)
        for group in order:
            blocks = [
                next_rows(bnd[b, d], factor, older).astype(jnp.bfloat16)
                for d, _ in group for b in range(nb)
            ]
            for at, (d, _) in enumerate(group):
                for b in range(nb):
                    snd[step + 1, d * nb + b] = blocks[at * nb + b]
            for d, target in group:
                exchange(step + 1, d, target).start()

        def keep(r, value):
            y[older, r] = value
            vb[r] = value.astype(jnp.bfloat16)

        lagged(lambda r: next_rows(r, factor, older), keep)
        local_product()
        return carry

    lax.fori_loop(0, DEG - 1, advance, 0)

    last, older = DEG - 1, DEG % 2
    receive(last)
    k = y.shape[2]

    def keep_last(r, value):
        y[older, r] = value
        high = value.astype(jnp.bfloat16)
        stk[0:k, r * bs:(r + 1) * bs] = high
        stk[k:2 * k, r * bs:(r + 1) * bs] = (value - high.astype(jnp.float32)).astype(jnp.bfloat16)

    lagged(lambda r: next_rows(r, 2.0, older), keep_last)
    store_y = pltpu.make_async_copy(y.at[older], y_hbm, out_sem)
    store_y.start()
    both = dot_nt(stk[...], stk[...])
    both = both[0:k] + both[k:2 * k]
    raw = both[:, 0:k] + both[:, k:2 * k]
    half = k // 2

    def all_sum(part, buf, axis, here, count, send_sems, recv_sems):
        buf[here] = part
        copies = []
        for off in range(1, count):
            down, up = count - off, off - 1
            peer = jnp.where(
                2 * here < count,
                down - jnp.where(down <= here, 1, 0),
                up + jnp.where(up >= here, 1, 0),
            )
            copy = pltpu.make_async_remote_copy(
                src_ref=buf.at[here],
                dst_ref=buf.at[here],
                send_sem=send_sems.at[off],
                recv_sem=recv_sems.at[here],
                device_id={axis: peer},
                device_id_type=MESH,
            )
            copy.start()
            copies.append(copy)
        for off in range(1, count):
            other = lax.rem(here + off, count)
            pltpu.make_async_remote_copy(
                src_ref=buf.at[other],
                dst_ref=buf.at[other],
                send_sem=send_sems.at[off],
                recv_sem=recv_sems.at[other],
                device_id={axis: other},
                device_id_type=MESH,
            ).wait_recv()
        total = buf[0]
        for other in range(1, count):
            total = total + buf[other]
        return total, copies

    packed = jnp.concatenate([raw[0:half], raw[half:k]], axis=1)
    row_sum, copies_x = all_sum(packed, gx, "px", i, n_px, gx_snd, gx_rcv)
    total, copies_y = all_sum(row_sum, gy, "py", j, n_py, gy_snd, gy_rcv)
    g_out[...] = total

    for copy in copies_x + copies_y:
        copy.wait_send()

    def drain(step, carry):
        for d in range(4):
            exchange(step, d).wait_send()
        return carry

    lax.fori_loop(0, DEG, drain, 0)
    store_y.wait()


def scale_kernel(total_rows, y_hbm, g_hbm, f_hbm, gram_hbm, y, f, g_ref, gram_ref, in_sem, out_sem):
    rows = y.shape[0] // CHUNKS
    parts = [pl.ds(c * rows, rows) for c in range(CHUNKS)]
    loads = [pltpu.make_async_copy(y_hbm.at[p], y.at[p], in_sem.at[c]) for c, p in enumerate(parts)]
    stores = [pltpu.make_async_copy(f.at[p], f_hbm.at[p], out_sem.at[c]) for c, p in enumerate(parts)]
    load_g = pltpu.make_async_copy(g_hbm, g_ref, in_sem.at[CHUNKS])
    store_g = pltpu.make_async_copy(gram_ref, gram_hbm, out_sem.at[CHUNKS])
    load_g.start()
    for load in loads:
        load.start()
    load_g.wait()
    half = g_ref.shape[0]
    k = 2 * half
    g = g_ref[...]
    raw = jnp.concatenate([g[:, 0:k], g[:, k:2 * k]], axis=0)
    on_diag = lax.broadcasted_iota(jnp.int32, (k, k), 0) == lax.broadcasted_iota(
        jnp.int32, (k, k), 1
    )
    diag = jnp.where(on_diag, raw, 0.0)
    scale_col = lax.rsqrt(jnp.sum(diag, axis=1, keepdims=True) / total_rows + 1e-06)
    scale_row = lax.rsqrt(jnp.sum(diag, axis=0, keepdims=True) / total_rows + 1e-06)
    gram = raw * scale_col * scale_row / total_rows
    gram_ref[...] = jnp.where((scale_col == 0.0) | (scale_row == 0.0), 0.0, gram)
    store_g.start()
    for c, p in enumerate(parts):
        loads[c].wait()
        f[p] = y[p] * scale_col[None]
        stores[c].start()
    for store in stores:
        store.wait()
    store_g.wait()


def shards(n_px, n_py, start_vecs, local_tiles, local_cols, halo_tiles, halo_slot, boundary):
    rb, k, bs = start_vecs.shape
    nb = boundary.shape[1]
    total_rows = rb * bs * n_px * n_py
    f32, bf16 = jnp.float32, jnp.bfloat16
    smem = pl.BlockSpec(memory_space=pltpu.SMEM)
    vmem = pl.BlockSpec(memory_space=pltpu.VMEM)
    anywhere = pl.BlockSpec(memory_space=pl.ANY)
    dma = pltpu.SemaphoreType.DMA
    flops = 2 * DEG * rb * (local_cols.shape[1] + 1) * k * bs * bs
    vecs, gram_sum = pl.pallas_call(
        functools.partial(filter_kernel, n_px, n_py),
        out_shape=(
            jax.ShapeDtypeStruct((rb, k, bs), f32),
            jax.ShapeDtypeStruct((k // 2, 2 * k), f32),
        ),
        in_specs=[smem, smem, smem, anywhere, anywhere, anywhere],
        out_specs=(anywhere, vmem),
        scratch_shapes=[
            pltpu.VMEM((2, rb, k, bs), f32),
            pltpu.VMEM((rb, k, bs), bf16),
            pltpu.VMEM((rb, k, bs), f32),
            pltpu.VMEM(local_tiles.shape, bf16),
            pltpu.VMEM(halo_tiles.shape, bf16),
            pltpu.VMEM((rb, local_cols.shape[1] * bs, bs), bf16),
            pltpu.VMEM(halo_tiles.shape, bf16),
            pltpu.VMEM((DEG, 4 * nb, k, bs), bf16),
            pltpu.VMEM((DEG, 4 * nb, k, bs), bf16),
            pltpu.VMEM((4 * nb, k, bs), bf16),
            pltpu.VMEM((2 * k, rb * bs), bf16),
            pltpu.VMEM((n_px, k // 2, 2 * k), f32),
            pltpu.VMEM((n_py, k // 2, 2 * k), f32),
            dma((3,)),
            dma,
            dma((DEG, 4)),
            dma((DEG, 4)),
            dma((n_px,)),
            dma((n_px,)),
            dma((n_py,)),
            dma((n_py,)),
        ],
        compiler_params=pltpu.CompilerParams(
            collective_id=0, has_side_effects=True, vmem_limit_bytes=VMEM_BYTES
        ),
        cost_estimate=pl.CostEstimate(
            flops=flops, bytes_accessed=4 * 1024 * 1024, transcendentals=0
        ),
    )(local_cols.T, halo_slot, boundary.T, start_vecs, local_tiles, halo_tiles)
    return pl.pallas_call(
        functools.partial(scale_kernel, total_rows),
        out_shape=(
            jax.ShapeDtypeStruct((rb, k, bs), f32),
            jax.ShapeDtypeStruct((k, k), f32),
        ),
        in_specs=[anywhere, anywhere],
        out_specs=(anywhere, anywhere),
        scratch_shapes=[
            pltpu.VMEM((rb, k, bs), f32),
            pltpu.VMEM((rb, k, bs), f32),
            pltpu.VMEM((k // 2, 2 * k), f32),
            pltpu.VMEM((k, k), f32),
            dma((CHUNKS + 1,)),
            dma((CHUNKS + 1,)),
        ],
        compiler_params=pltpu.CompilerParams(vmem_limit_bytes=VMEM_BYTES),
        cost_estimate=pl.CostEstimate(
            flops=rb * k * bs, bytes_accessed=2 * 4 * rb * k * bs, transcendentals=k
        ),
    )(vecs, gram_sum)


def solution(mesh):
    return jax.shard_map(
        functools.partial(shards, mesh.shape["px"], mesh.shape["py"]),
        mesh=mesh,
        in_specs=(
            P(("px", "py"), None, None),
            P(("px", "py"), None, None, None),
            P(("px", "py"), None),
            P(("px", "py"), None, None),
            P(("px", "py")),
            P(("px", "py"), None),
        ),
        out_specs=(P(("px", "py"), None, None), P()),
        check_vma=False,
    )
```
